32 devices in a mesh: left: 8 (over y, x, core), right: 4 (over z).
Axes of the slice: x: 2, y: 2, z: 4, core: 2. Of those that a mesh axis runs over, the one named last changes fastest.
Arguments:
- corner: bfloat16 [32, 256, 256], P(('left', 'right')), may hold values from -6 to 6
- edge_row: bfloat16 [64, 32, 256, 256], P('left', 'right'), may hold values from -0.0625 to 0.0625
- source_row: int32 [64, 32], P('left', 'right'), may hold values from 0 to 31, as said below
- proj_row: bfloat16 [64, 256, 256], P('left'), may hold values from -0.375 to 0.375
- edge_col: bfloat16 [16, 80, 256, 256], P('right', 'left'), may hold values from -0.0390625 to 0.0390625
- source_col: int32 [16, 80], P('right', 'left'), may hold values from 0 to 63, as said below
- proj_col: bfloat16 [16, 256, 256], P('right'), may hold values from -0.375 to 0.375
Outputs:
- absorbed_row: bfloat16 [64, 256, 256], P(('left', 'right'))
- new_corner: bfloat16 [16, 256, 256], P('right', 'left')
The draws below stay inside these ranges and needn't reach their ends.
Inputs may be any that keep to these rules, and one draw needn't show every extreme that they name: source_row[f, j] is a sector whose block lies on a device with right index j // 8, that is (source_row[f, j]) % 4 == j // 8. source_col[g, j] is a sector of the left index j // 10: source_col[g, j] // 8 == j // 10.
All inputs are finite; a program needn't handle non-finite values.
Results may differ from the reference program's by a relative error of at most 0.03.
Values may be sent and summed in bfloat16 or wider, within the bound.
A program may use at most 128 MiB of HBM per device.

```python
import jax
import jax.numpy as jnp
from jax import lax

P_SIZE = 256
SEC_DEV = 1
O1 = 2
K1 = 8
K2 = 10
NSEC = 32
NOUT1 = 64
KF1 = 32
NOUT2 = 16
KF2 = 80
N_LEFT = 8
N_RIGHT = 4


def draw_source_row(key, part):
    key_left = jax.random.fold_in(key, 11)
    key_local = jax.random.fold_in(key, 12)
    left_pick = jax.random.randint(key_left, (NOUT1, KF1), 0, N_LEFT)
    local_pick = jax.random.randint(key_local, (NOUT1, KF1), 0, SEC_DEV)
    right_owner = (jnp.arange(KF1, dtype=jnp.int32) // K1)[None, :]
    values = left_pick * (N_RIGHT * SEC_DEV) + right_owner * SEC_DEV + local_pick
    values = values.at[0, 0].set(0)
    values = values.at[NOUT1 - 1, KF1 - 1].set(NSEC - 1)
    return values.astype(jnp.int32)


def draw_source_col(key, part):
    key_pick = jax.random.fold_in(key, 21)
    inner_pick = jax.random.randint(key_pick, (NOUT2, KF2), 0, O1 * N_RIGHT)
    left_owner = (jnp.arange(KF2, dtype=jnp.int32) // K2)[None, :]
    values = left_owner * (O1 * N_RIGHT) + inner_pick
    values = values.at[0, 0].set(0)
    values = values.at[NOUT2 - 1, KF2 - 1].set(NOUT1 - 1)
    return values.astype(jnp.int32)


def levels(stream_key, dims, shards, smallest, top_value):
    factor_of, own = 1.0, jax.random.fold_in(stream_key, 6)
    for dim, parts in shards:
        steps = jnp.exp(jax.random.uniform(jax.random.fold_in(own, dim), (parts,), jnp.float32, smallest / len(shards), top_value / len(shards)))
        factor_of = factor_of * jnp.repeat(steps, dims[dim] // parts).reshape([-1 if axis == dim else 1 for axis in range(len(dims))])
    return factor_of


def normal_values(stream_key, shape, deviation, most, pieces=(), held_as=jnp.bfloat16):
    level = levels(stream_key, shape, pieces, -0.22, 0.18) if pieces else 1.0
    values = jax.random.normal(stream_key, shape, jnp.float32) * deviation * level
    return jnp.minimum(jnp.maximum(values, -most), most).astype(held_as)


def setup_inputs(seed: int = 0) -> dict:
    key_list = jax.random.split(jax.random.key(seed), 8)
    corner = normal_values(key_list[0], (NSEC, P_SIZE, P_SIZE), 1.0, 6.0, ((0, 32),))
    edge_row = normal_values(key_list[1], (NOUT1, KF1, P_SIZE, P_SIZE), (P_SIZE * KF1) ** -0.5, 0.0625, ((0, 8), (1, 4)))
    source_row = draw_source_row(jax.random.fold_in(key_list[7], 71), 0)
    proj_row = normal_values(key_list[3], (NOUT1, P_SIZE, P_SIZE), P_SIZE ** -0.5, 0.375, ((0, 8),))
    edge_col = normal_values(key_list[4], (NOUT2, KF2, P_SIZE, P_SIZE), (P_SIZE * KF2) ** -0.5, 0.0390625, ((0, 4), (1, 8)))
    source_col = draw_source_col(jax.random.fold_in(key_list[7], 71), 0)
    proj_col = normal_values(key_list[6], (NOUT2, P_SIZE, P_SIZE), P_SIZE ** -0.5, 0.375, ((0, 4),))
    return dict(corner=corner, edge_row=edge_row, source_row=source_row, proj_row=proj_row, edge_col=edge_col, source_col=source_col, proj_col=proj_col)


def reference(corner, edge_row, source_row, proj_row, edge_col, source_col, proj_col):
    def row_one(items):
        index_list, edges, projector = items
        blocks = jnp.take(corner, index_list, axis=0).astype(jnp.float32)
        row_sum = jnp.einsum("kab,kbc->ac", blocks, edges.astype(jnp.float32)).astype(jnp.bfloat16)
        return jnp.dot(projector.T, row_sum, preferred_element_type=jnp.float32).astype(jnp.bfloat16)

    absorbed_row = lax.map(row_one, (source_row, edge_row, proj_row))

    def col_one(items):
        index_list, edges, projector = items
        blocks = jnp.take(absorbed_row, index_list, axis=0).astype(jnp.float32)
        col_sum = jnp.einsum("kab,kbc->ac", edges.astype(jnp.float32), blocks).astype(jnp.bfloat16)
        return jnp.dot(col_sum, projector, preferred_element_type=jnp.float32).astype(jnp.bfloat16)

    new_corner = lax.map(col_one, (source_col, edge_col, proj_col))
    return absorbed_row, new_corner
```

```python
import functools

import jax
import jax.numpy as jnp
from jax import lax
from jax.experimental import pallas as pl
from jax.experimental.pallas import tpu as pltpu
from jax.sharding import PartitionSpec as P

MESH = pl.DeviceIdType.MESH
PARTS = 2
LAG = 4


def wait_bytes(ref, sem):
    pltpu.make_async_copy(ref, ref, sem).wait()


def kernel(
    n_left, n_right,
    source_row, source_col, corner, edge_row, proj_row, edge_col, proj_col,
    absorbed_out, corner_out,
    gathered_0, gathered_1, edges_1, edges_2, projs_1, projs_2,
    own, prefix, suffix, to_right, to_left, row_sum, absorbed, col_part, col_in,
    edge_sem_1, edge_sem_2, proj_sem, local_sem,
    peer_send, peer_recv, pair_send, pair_recv,
    right_send, right_recv, left_send, left_recv, col_send, col_recv,
):
    held = corner.shape[0]
    size = corner.shape[1]
    half = size // PARTS
    sectors, entries_1 = source_row.shape
    groups, entries_2 = source_col.shape
    mine = absorbed_out.shape[0]
    chips = n_left // 2
    per_col = PARTS * sectors
    steps = PARTS * per_col
    depth = LAG * (n_right - 1)
    l, r = lax.axis_index("left"), lax.axis_index("right")
    core, chip = lax.rem(l, 2), lax.div(l, 2)
    gathered = (gathered_0, gathered_1)

    corner_copies = [
        pltpu.make_async_copy(
            corner.at[:, pl.ds(a * half, half), :], gathered[a].at[core, chip], local_sem.at[a])
        for a in range(PARTS)
    ]
    for copy in corner_copies:
        copy.start()

    @pl.loop(0, sectors)
    def _(f):
        pltpu.make_async_copy(edge_row.at[f], edges_1.at[f], edge_sem_1.at[f]).start()

    load_1 = pltpu.make_async_copy(proj_row, projs_1, proj_sem.at[0])
    load_1.start()

    @pl.loop(0, groups)
    def _(g):
        pltpu.make_async_copy(edge_col.at[g], edges_2.at[g], edge_sem_2.at[g]).start()

    load_2 = pltpu.make_async_copy(proj_col, projs_2, proj_sem.at[1])
    load_2.start()

    barrier = pltpu.get_barrier_semaphore()
    for off in range(1, n_left):
        pl.semaphore_signal(
            barrier, inc=1, device_id=(lax.rem(l + off, n_left), r), device_id_type=MESH)

    @pl.when(r > 0)
    def _():
        pl.semaphore_signal(barrier, inc=1, device_id=(l, r - 1), device_id_type=MESH)

    @pl.when(r < n_right - 1)
    def _():
        pl.semaphore_signal(barrier, inc=1, device_id=(l, r + 1), device_id_type=MESH)

    pl.semaphore_wait(
        barrier,
        n_left - 1 + jnp.where(r > 0, 1, 0) + jnp.where(r < n_right - 1, 1, 0))

    for a in range(PARTS):
        for off in range(1, chips):
            peer = lax.rem(chip + off, chips)
            pltpu.make_async_remote_copy(
                src_ref=corner.at[:, pl.ds(a * half, half), :],
                dst_ref=gathered[a].at[core, chip],
                send_sem=peer_send.at[a], recv_sem=peer_recv.at[a],
                device_id=(peer * 2 + core, r), device_id_type=MESH).start()

    def pair_copy(a):
        return pltpu.make_async_remote_copy(
            src_ref=gathered[a].at[core], dst_ref=gathered[a].at[core],
            send_sem=pair_send.at[a], recv_sem=pair_recv.at[a],
            device_id=(chip * 2 + 1 - core, r), device_id_type=MESH)

    def forward(a):
        corner_copies[a].wait()
        if chips > 1:
            wait_bytes(gathered[a].at[0, pl.ds(0, chips - 1)], peer_recv.at[a])
        pair_copy(a).start()

    @pl.when(r == 0)
    def _():
        prefix[...] = jnp.zeros_like(prefix)

    @pl.when(r == n_right - 1)
    def _():
        suffix[...] = jnp.zeros_like(suffix)

    def row_product(step, a):
        f = step - a * sectors
        if a == 0:
            wait_bytes(edges_1.at[f], edge_sem_1.at[f])
        total = None
        for k in range(entries_1):
            source = source_row[f, k]
            owner = lax.div(source, held * n_right)
            block = gathered[a][lax.rem(owner, 2), lax.div(owner, 2), lax.rem(source, held)]
            term = jnp.dot(block, edges_1[f, k], preferred_element_type=jnp.float32)
            total = term if total is None else total + term
        for c in range(PARTS):
            own[step + c * per_col] = total[:, c * half:(c + 1) * half]

    def travel(i):
        x = i - LAG * r

        @pl.when((x >= 0) & (x < steps))
        def _():
            @pl.when(r > 0)
            def _():
                wait_bytes(prefix.at[x], right_recv.at[x])

            @pl.when(r < n_right - 1)
            def _():
                to_right[x] = (prefix[x].astype(jnp.float32) + own[x]).astype(jnp.bfloat16)
                pltpu.make_async_remote_copy(
                    src_ref=to_right.at[x], dst_ref=prefix.at[x],
                    send_sem=right_send, recv_sem=right_recv.at[x],
                    device_id=(l, r + 1), device_id_type=MESH).start()

        y = i - LAG * (n_right - 1 - r)

        @pl.when((y >= 0) & (y < steps))
        def _():
            @pl.when(r < n_right - 1)
            def _():
                wait_bytes(suffix.at[y], left_recv.at[y])

            @pl.when(r > 0)
            def _():
                to_left[y] = (suffix[y].astype(jnp.float32) + own[y]).astype(jnp.bfloat16)
                pltpu.make_async_remote_copy(
                    src_ref=to_left.at[y], dst_ref=suffix.at[y],
                    send_sem=left_send, recv_sem=left_recv.at[y],
                    device_id=(l, r - 1), device_id_type=MESH).start()

        t = i - depth

        @pl.when((t >= 0) & (t < steps))
        def _():
            c, a, f = t // per_col, (t // sectors) % PARTS, t % sectors
            whole = prefix[t].astype(jnp.float32) + own[t] + suffix[t].astype(jnp.float32)
            row_sum[f, a] = whole.astype(jnp.bfloat16)

            @pl.when(a == PARTS - 1)
            def _():
                value = lax.dot_general(
                    projs_1[f], row_sum[f].reshape(size, half), (((0,), (0,)), ((), ())),
                    preferred_element_type=jnp.float32)
                absorbed[c, f] = value.astype(jnp.bfloat16)

    def column(c, g):
        if c == 0:
            wait_bytes(edges_2.at[g], edge_sem_2.at[g])
        total = None
        for k in range(entries_2):
            block = absorbed[c, lax.rem(source_col[g, k], sectors)]
            term = jnp.dot(edges_2[g, k], block, preferred_element_type=jnp.float32)
            total = term if total is None else total + term
        col_part[c, g] = total.astype(jnp.bfloat16).reshape(n_left, size // n_left, half)
        for off in range(1, n_left):
            there = lax.rem(l + off, n_left)
            pltpu.make_async_remote_copy(
                src_ref=col_part.at[c, g, there], dst_ref=col_in.at[c, g, l],
                send_sem=col_send, recv_sem=col_recv.at[c, g],
                device_id=(there, r), device_id_type=MESH).start()
        col_in[c, g, l] = col_part[c, g, l]

    forward(0)
    pair_copy(0).wait_recv()

    @pl.loop(0, sectors)
    def _(i):
        row_product(i, 0)
        travel(i)

        @pl.when(i == sectors // 2)
        def _():
            forward(1)

    pair_copy(1).wait_recv()

    load_1.wait()

    @pl.loop(sectors, per_col)
    def _(i):
        row_product(i, 1)
        travel(i)

    first = depth + per_col

    @pl.loop(per_col, steps + depth)
    def _(i):
        travel(i)

        @pl.when((i >= first) & (i < first + groups))
        def _():
            column(0, i - first)

    @pl.loop(0, groups)
    def _(g):
        column(1, g)

    for o in range(mine):
        for c in range(PARTS):
            absorbed_out[o, :, c * half:(c + 1) * half] = absorbed[c, r * mine + o]

    load_2.wait()

    @pl.loop(0, groups)
    def _(g):
        parts = []
        for c in range(PARTS):
            wait_bytes(col_in.at[c, g, pl.ds(0, n_left - 1)], col_recv.at[c, g])
            parts.append(jnp.sum(col_in[c, g].astype(jnp.float32), axis=0).astype(jnp.bfloat16))
        corner_out[g] = jnp.dot(
            jnp.concatenate(parts, axis=1), projs_2[g], preferred_element_type=jnp.float32
        ).astype(jnp.bfloat16)

    for a in range(PARTS):
        if chips > 1:
            wait_bytes(gathered[a].at[0, pl.ds(0, chips - 1)], peer_send.at[a])
        pair_copy(a).wait_send()

    @pl.when(r < n_right - 1)
    def _():
        wait_bytes(to_right, right_send)

    @pl.when(r > 0)
    def _():
        wait_bytes(to_left, left_send)

    wait_bytes(col_part.at[:, :, pl.ds(0, n_left - 1)], col_send)


def body(n_left, n_right, corner, edge_row, source_row, proj_row, edge_col, source_col, proj_col):
    held, size, _ = corner.shape
    sectors, entries_1 = source_row.shape
    groups, entries_2 = source_col.shape
    half = size // PARTS
    chips = n_left // 2
    steps = PARTS * PARTS * sectors
    rows = size // n_left
    bf16 = jnp.bfloat16
    dma = pltpu.SemaphoreType.DMA
    vmem = pl.BlockSpec(memory_space=pltpu.VMEM)
    smem = pl.BlockSpec(memory_space=pltpu.SMEM)
    far = pl.BlockSpec(memory_space=pl.ANY)
    gathered = pltpu.VMEM((2, chips, held, half, size), bf16)
    pieces = pltpu.VMEM((steps, half, half), bf16)
    columns = pltpu.VMEM((PARTS, groups, n_left, rows, half), bf16)
    return pl.pallas_call(
        functools.partial(kernel, n_left, n_right),
        out_shape=(
            jax.ShapeDtypeStruct((sectors // n_right, size, size), bf16),
            jax.ShapeDtypeStruct((groups, rows, size), bf16),
        ),
        in_specs=[smem, smem, far, far, far, far, far],
        out_specs=(vmem, vmem),
        scratch_shapes=[
            gathered, gathered,
            pltpu.VMEM(edge_row.shape, bf16), pltpu.VMEM(edge_col.shape, bf16),
            pltpu.VMEM(proj_row.shape, bf16), pltpu.VMEM(proj_col.shape, bf16),
            pltpu.VMEM((steps, half, half), jnp.float32),
            pieces, pieces, pieces, pieces,
            pltpu.VMEM((sectors, PARTS, half, half), bf16),
            pltpu.VMEM((PARTS, sectors, size, half), bf16),
            columns, columns,
            dma((sectors,)), dma((groups,)), dma((2,)), dma((PARTS,)),
            dma((PARTS,)), dma((PARTS,)), dma((PARTS,)), dma((PARTS,)),
            dma, dma((steps,)), dma, dma((steps,)), dma, dma((PARTS, groups)),
        ],
        compiler_params=pltpu.CompilerParams(
            collective_id=0, has_side_effects=True, vmem_limit_bytes=58 * 2**20),
        cost_estimate=pl.CostEstimate(
            flops=2 * size**3 * (sectors * (entries_1 + 1) + groups * (entries_2 + 1)),
            bytes_accessed=2 * (edge_row.size + edge_col.size + proj_row.size + proj_col.size),
            transcendentals=0),
    )(source_row, source_col, corner, edge_row, proj_row, edge_col, proj_col)


def solution(mesh):
    in_specs = (
        P(("left", "right"), None, None),
        P("left", "right", None, None),
        P("left", "right"),
        P("left", None, None),
        P("right", "left", None, None),
        P("right", "left"),
        P("right", None, None),
    )
    out_specs = (P(("left", "right"), None, None), P("right", "left", None))
    return jax.shard_map(
        functools.partial(body, mesh.shape["left"], mesh.shape["right"]),
        mesh=mesh, in_specs=in_specs, out_specs=out_specs, check_vma=False)
```

```python
import functools

import jax
import jax.numpy as jnp
from jax import lax
from jax.experimental import pallas as pl
from jax.experimental.pallas import tpu as pltpu
from jax.sharding import PartitionSpec as P

MESH = pl.DeviceIdType.MESH
PARTS = 2
LAGS = (2, 4)
SLICES = 2


def wait_bytes(ref, sem):
    pltpu.make_async_copy(ref, ref, sem).wait()


def kernel(
    n_left, n_right,
    source_row, source_col, corner, edge_row, proj_row, edge_col, proj_col,
    absorbed_out, corner_out,
    gathered_0, gathered_1, edges_1, edges_2, projs_1, projs_2,
    own, prefix, suffix, to_right, to_left, row_sum, absorbed, col_total, col_part, col_in,
    edge_sem_1, edge_sem_2, proj_sem, local_sem,
    peer_send, peer_recv, pair_send, pair_recv,
    right_send, right_recv, left_send, left_recv, col_send, col_recv,
):
    held = corner.shape[0]
    size = corner.shape[1]
    half = size // PARTS
    sectors, entries_1 = source_row.shape
    groups, entries_2 = source_col.shape
    mine = absorbed_out.shape[0]
    chips = n_left // 2
    per_col = PARTS * sectors
    steps = PARTS * per_col
    l, r = lax.axis_index("left"), lax.axis_index("right")
    core, chip = lax.rem(l, 2), lax.div(l, 2)
    gathered = (gathered_0, gathered_1)

    corner_copies = [
        pltpu.make_async_copy(
            corner.at[:, pl.ds(a * half, half), :], gathered[a].at[core, chip], local_sem.at[a])
        for a in range(PARTS)
    ]
    for copy in corner_copies:
        copy.start()

    load_1 = pltpu.make_async_copy(proj_row, projs_1, proj_sem.at[0])
    load_1.start()

    @pl.loop(0, sectors)
    def _(f):
        pltpu.make_async_copy(edge_row.at[f], edges_1.at[f], edge_sem_1.at[f]).start()

    @pl.loop(0, groups)
    def _(g):
        pltpu.make_async_copy(edge_col.at[g], edges_2.at[g], edge_sem_2.at[g]).start()

    load_2 = pltpu.make_async_copy(proj_col, projs_2, proj_sem.at[1])
    load_2.start()

    barrier = pltpu.get_barrier_semaphore()
    for off in range(1, n_left):
        pl.semaphore_signal(
            barrier, inc=1, device_id=(lax.rem(l + off, n_left), r), device_id_type=MESH)

    @pl.when(r > 0)
    def _():
        pl.semaphore_signal(barrier, inc=1, device_id=(l, r - 1), device_id_type=MESH)

    @pl.when(r < n_right - 1)
    def _():
        pl.semaphore_signal(barrier, inc=1, device_id=(l, r + 1), device_id_type=MESH)

    pl.semaphore_wait(
        barrier,
        n_left - 1 + jnp.where(r > 0, 1, 0) + jnp.where(r < n_right - 1, 1, 0))

    for a in range(PARTS):
        for off in range(1, chips):
            peer = lax.rem(chip + off, chips)
            pltpu.make_async_remote_copy(
                src_ref=corner.at[:, pl.ds(a * half, half), :],
                dst_ref=gathered[a].at[core, chip],
                send_sem=peer_send.at[a], recv_sem=peer_recv.at[a],
                device_id=(peer * 2 + core, r), device_id_type=MESH).start()

    def pair_copy(a):
        return pltpu.make_async_remote_copy(
            src_ref=gathered[a].at[core], dst_ref=gathered[a].at[core],
            send_sem=pair_send.at[a], recv_sem=pair_recv.at[a],
            device_id=(chip * 2 + 1 - core, r), device_id_type=MESH)

    def forward(a):
        corner_copies[a].wait()
        if chips > 1:
            wait_bytes(gathered[a].at[0, pl.ds(0, chips - 1)], peer_recv.at[a])
        pair_copy(a).start()

    @pl.when(r == 0)
    def _():
        prefix[...] = jnp.zeros_like(prefix)

    @pl.when(r == n_right - 1)
    def _():
        suffix[...] = jnp.zeros_like(suffix)

    def row_product(step, a):
        f = step - a * sectors
        if a == 0:
            wait_bytes(edges_1.at[f], edge_sem_1.at[f])
        total = None
        for k in range(entries_1):
            source = source_row[f, k]
            owner = lax.div(source, held * n_right)
            block = gathered[a][lax.rem(owner, 2), lax.div(owner, 2), lax.rem(source, held)]
            term = jnp.dot(block, edges_1[f, k], preferred_element_type=jnp.float32)
            total = term if total is None else total + term
        for c in range(PARTS):
            own[step + c * per_col] = total[:, c * half:(c + 1) * half]

    def piece(i, hops):
        early, late = i - LAGS[0] * hops, i - LAGS[1] * hops
        valid = ((early >= 0) & (early < per_col)) | ((late >= per_col) & (late < steps))
        return jnp.where(early < per_col, early, late), valid

    def travel(i):
        x, valid_x = piece(i, r)

        @pl.when(valid_x)
        def _():
            @pl.when(r > 0)
            def _():
                wait_bytes(prefix.at[x], right_recv.at[x])

            @pl.when(r < n_right - 1)
            def _():
                to_right[x] = (prefix[x].astype(jnp.float32) + own[x]).astype(jnp.bfloat16)
                pltpu.make_async_remote_copy(
                    src_ref=to_right.at[x], dst_ref=prefix.at[x],
                    send_sem=right_send, recv_sem=right_recv.at[x],
                    device_id=(l, r + 1), device_id_type=MESH).start()

        y, valid_y = piece(i, n_right - 1 - r)

        @pl.when(valid_y)
        def _():
            @pl.when(r < n_right - 1)
            def _():
                wait_bytes(suffix.at[y], left_recv.at[y])

            @pl.when(r > 0)
            def _():
                to_left[y] = (suffix[y].astype(jnp.float32) + own[y]).astype(jnp.bfloat16)
                pltpu.make_async_remote_copy(
                    src_ref=to_left.at[y], dst_ref=suffix.at[y],
                    send_sem=left_send, recv_sem=left_recv.at[y],
                    device_id=(l, r - 1), device_id_type=MESH).start()

        t, valid_t = piece(i, n_right - 1)

        @pl.when(valid_t)
        def _():
            c, a, f = t // per_col, (t // sectors) % PARTS, t % sectors
            whole = prefix[t].astype(jnp.float32) + own[t] + suffix[t].astype(jnp.float32)
            row_sum[f, a] = whole.astype(jnp.bfloat16)

            @pl.when(a == PARTS - 1)
            def _():
                value = jnp.dot(
                    projs_1[f], row_sum[f].reshape(size, half),
                    preferred_element_type=jnp.float32)
                absorbed[c, f] = value.astype(jnp.bfloat16)

    def column_sum(c, g, ks):
        total = None
        for k in ks:
            block = absorbed[c, lax.rem(source_col[g, k], sectors)]
            term = jnp.dot(edges_2[g, k], block, preferred_element_type=jnp.float32)
            total = term if total is None else total + term
        return total

    def column_send(c, g, total):
        col_part[c, g] = total.astype(jnp.bfloat16).reshape(n_left, size // n_left, half)
        for off in range(1, n_left):
            there = lax.rem(l + off, n_left)
            pltpu.make_async_remote_copy(
                src_ref=col_part.at[c, g, there], dst_ref=col_in.at[c, g, l],
                send_sem=col_send, recv_sem=col_recv.at[c, g],
                device_id=(there, r), device_id_type=MESH).start()
        col_in[c, g, l] = col_part[c, g, l]

    load_1.wait()

    @pl.loop(0, sectors)
    def _(f):
        projs_1[f] = projs_1[f].T

    forward(0)
    pair_copy(0).wait_recv()

    @pl.loop(0, sectors)
    def _(i):
        row_product(i, 0)
        travel(i)

        @pl.when(i == sectors // 2)
        def _():
            forward(1)

    pair_copy(1).wait_recv()

    @pl.loop(sectors, per_col)
    def _(i):
        row_product(i, 1)
        travel(i)

    first = per_col + LAGS[0] * (n_right - 1)
    cuts = [entries_2 * n // SLICES for n in range(SLICES + 1)]

    @pl.loop(per_col, steps + LAGS[1] * (n_right - 1))
    def _(i):
        travel(i)
        turn = i - first

        for n in range(SLICES):
            @pl.when((turn >= 0) & (turn < SLICES * groups) & (turn % SLICES == n))
            def _():
                g = turn // SLICES
                if n == 0:
                    wait_bytes(edges_2.at[g], edge_sem_2.at[g])
                total = column_sum(0, g, range(cuts[n], cuts[n + 1]))
                if n > 0:
                    total = total + col_total[...]
                if n < SLICES - 1:
                    col_total[...] = total
                else:
                    column_send(0, g, total)

    @pl.loop(0, groups)
    def _(g):
        column_send(1, g, column_sum(1, g, range(entries_2)))

    for o in range(mine):
        for c in range(PARTS):
            absorbed_out[o, :, c * half:(c + 1) * half] = absorbed[c, r * mine + o]

    load_2.wait()

    @pl.loop(0, groups)
    def _(g):
        parts = []
        for c in range(PARTS):
            wait_bytes(col_in.at[c, g, pl.ds(0, n_left - 1)], col_recv.at[c, g])
            parts.append(jnp.sum(col_in[c, g].astype(jnp.float32), axis=0).astype(jnp.bfloat16))
        corner_out[g] = jnp.dot(
            jnp.concatenate(parts, axis=1), projs_2[g], preferred_element_type=jnp.float32
        ).astype(jnp.bfloat16)

    for a in range(PARTS):
        if chips > 1:
            wait_bytes(gathered[a].at[0, pl.ds(0, chips - 1)], peer_send.at[a])
        pair_copy(a).wait_send()

    @pl.when(r < n_right - 1)
    def _():
        wait_bytes(to_right, right_send)

    @pl.when(r > 0)
    def _():
        wait_bytes(to_left, left_send)

    wait_bytes(col_part.at[:, :, pl.ds(0, n_left - 1)], col_send)


def hand_over(a, b, a_out, b_out, sem):
    copies = [pltpu.make_async_copy(a, a_out, sem.at[0]), pltpu.make_async_copy(b, b_out, sem.at[1])]
    for copy in copies:
        copy.start()
    for copy in copies:
        copy.wait()


def body(n_left, n_right, corner, edge_row, source_row, proj_row, edge_col, source_col, proj_col):
    held, size, _ = corner.shape
    sectors, entries_1 = source_row.shape
    groups, entries_2 = source_col.shape
    half = size // PARTS
    chips = n_left // 2
    steps = PARTS * PARTS * sectors
    rows = size // n_left
    bf16 = jnp.bfloat16
    dma = pltpu.SemaphoreType.DMA
    vmem = pl.BlockSpec(memory_space=pltpu.VMEM)
    smem = pl.BlockSpec(memory_space=pltpu.SMEM)
    far = pl.BlockSpec(memory_space=pl.ANY)
    gathered = pltpu.VMEM((2, chips, held, half, size), bf16)
    pieces = pltpu.VMEM((steps, half, half), bf16)
    columns = pltpu.VMEM((PARTS, groups, n_left, rows, half), bf16)
    found = pl.pallas_call(
        functools.partial(kernel, n_left, n_right),
        out_shape=(
            jax.ShapeDtypeStruct((sectors // n_right, size, size), bf16),
            jax.ShapeDtypeStruct((groups, rows, size), bf16),
        ),
        in_specs=[smem, smem, far, far, far, far, far],
        out_specs=(vmem, vmem),
        scratch_shapes=[
            gathered, gathered,
            pltpu.VMEM(edge_row.shape, bf16), pltpu.VMEM(edge_col.shape, bf16),
            pltpu.VMEM(proj_row.shape, bf16), pltpu.VMEM(proj_col.shape, bf16),
            pltpu.VMEM((steps, half, half), jnp.float32),
            pieces, pieces, pieces, pieces,
            pltpu.VMEM((sectors, PARTS, half, half), bf16),
            pltpu.VMEM((PARTS, sectors, size, half), bf16),
            pltpu.VMEM((size, half), jnp.float32),
            columns, columns,
            dma((sectors,)), dma((groups,)), dma((2,)), dma((PARTS,)),
            dma((PARTS,)), dma((PARTS,)), dma((PARTS,)), dma((PARTS,)),
            dma, dma((steps,)), dma, dma((steps,)), dma, dma((PARTS, groups)),
        ],
        compiler_params=pltpu.CompilerParams(
            collective_id=0, has_side_effects=True, vmem_limit_bytes=58 * 2**20),
        cost_estimate=pl.CostEstimate(
            flops=2 * size**3 * (sectors * (entries_1 + 1) + groups * (entries_2 + 1)),
            bytes_accessed=2 * (edge_row.size + edge_col.size + proj_row.size + proj_col.size),
            transcendentals=0),
    )(source_row, source_col, corner, edge_row, proj_row, edge_col, proj_col)
    return pl.pallas_call(
        hand_over,
        out_shape=tuple(jax.ShapeDtypeStruct(x.shape, x.dtype) for x in found),
        in_specs=[far, far],
        out_specs=(far, far),
        scratch_shapes=[dma((2,))],
        compiler_params=pltpu.CompilerParams(vmem_limit_bytes=58 * 2**20),
        cost_estimate=pl.CostEstimate(
            flops=0, bytes_accessed=4 * sum(x.size for x in found), transcendentals=0),
    )(*found)


def solution(mesh):
    in_specs = (
        P(("left", "right"), None, None),
        P("left", "right", None, None),
        P("left", "right"),
        P("left", None, None),
        P("right", "left", None, None),
        P("right", "left"),
        P("right", None, None),
    )
    out_specs = (P(("left", "right"), None, None), P("right", "left", None))
    return jax.shard_map(
        functools.partial(body, mesh.shape["left"], mesh.shape["right"]),
        mesh=mesh, in_specs=in_specs, out_specs=out_specs, check_vma=False)
```

```python
import functools

import jax
import jax.numpy as jnp
from jax import lax
from jax.experimental import pallas as pl
from jax.experimental.pallas import tpu as pltpu
from jax.sharding import PartitionSpec as P

MESH = pl.DeviceIdType.MESH
PARTS = 2
LAGS = (4, 6)
SLICES = 2


def wait_bytes(ref, sem):
    pltpu.make_async_copy(ref, ref, sem).wait()


def kernel(
    n_left, n_right,
    source_row, source_col, corner, edge_row, proj_row, edge_col, proj_col,
    absorbed_out, corner_out,
    gathered_0, gathered_1, edges_1, edges_2, projs_1, projs_2,
    own, prefix, suffix, to_right, to_left, row_sum, absorbed, col_total, col_part, col_in,
    edge_sem_1, edge_sem_2, proj_sem, local_sem,
    peer_send, peer_recv, pair_send, pair_recv,
    right_send, right_recv, left_send, left_recv, col_send, col_recv,
):
    held = corner.shape[0]
    size = corner.shape[1]
    half = size // PARTS
    sectors, entries_1 = source_row.shape
    groups, entries_2 = source_col.shape
    mine = absorbed_out.shape[0]
    chips = n_left // 2
    per_col = PARTS * sectors
    steps = PARTS * per_col
    l, r = lax.axis_index("left"), lax.axis_index("right")
    core, chip = lax.rem(l, 2), lax.div(l, 2)
    gathered = (gathered_0, gathered_1)

    corner_copies = [
        pltpu.make_async_copy(
            corner.at[:, pl.ds(a * half, half), :], gathered[a].at[core, chip], local_sem.at[a])
        for a in range(PARTS)
    ]
    for copy in corner_copies:
        copy.start()

    load_1 = pltpu.make_async_copy(proj_row, projs_1, proj_sem.at[0])
    load_1.start()

    @pl.loop(0, sectors)
    def _(f):
        pltpu.make_async_copy(edge_row.at[f], edges_1.at[f], edge_sem_1.at[f]).start()

    @pl.loop(0, groups)
    def _(g):
        pltpu.make_async_copy(edge_col.at[g], edges_2.at[g], edge_sem_2.at[g]).start()

    load_2 = pltpu.make_async_copy(proj_col, projs_2, proj_sem.at[1])
    load_2.start()

    barrier = pltpu.get_barrier_semaphore()
    for off in range(1, n_left):
        pl.semaphore_signal(
            barrier, inc=1, device_id=(lax.rem(l + off, n_left), r), device_id_type=MESH)

    @pl.when(r > 0)
    def _():
        pl.semaphore_signal(barrier, inc=1, device_id=(l, r - 1), device_id_type=MESH)

    @pl.when(r < n_right - 1)
    def _():
        pl.semaphore_signal(barrier, inc=1, device_id=(l, r + 1), device_id_type=MESH)

    pl.semaphore_wait(
        barrier,
        n_left - 1 + jnp.where(r > 0, 1, 0) + jnp.where(r < n_right - 1, 1, 0))

    for a in range(PARTS):
        for off in range(1, chips):
            peer = lax.rem(chip + off, chips)
            pltpu.make_async_remote_copy(
                src_ref=corner.at[:, pl.ds(a * half, half), :],
                dst_ref=gathered[a].at[core, chip],
                send_sem=peer_send.at[a], recv_sem=peer_recv.at[a],
                device_id=(peer * 2 + core, r), device_id_type=MESH).start()

    def pair_copy(a):
        return pltpu.make_async_remote_copy(
            src_ref=gathered[a].at[core], dst_ref=gathered[a].at[core],
            send_sem=pair_send.at[a], recv_sem=pair_recv.at[a],
            device_id=(chip * 2 + 1 - core, r), device_id_type=MESH)

    def forward(a):
        corner_copies[a].wait()
        if chips > 1:
            wait_bytes(gathered[a].at[0, pl.ds(0, chips - 1)], peer_recv.at[a])
        pair_copy(a).start()

    @pl.when(r == 0)
    def _():
        prefix[...] = jnp.zeros_like(prefix)

    @pl.when(r == n_right - 1)
    def _():
        suffix[...] = jnp.zeros_like(suffix)

    def row_product(step, a):
        f = step - a * sectors
        if a == 0:
            wait_bytes(edges_1.at[f], edge_sem_1.at[f])
        total = None
        for k in range(entries_1):
            source = source_row[f, k]
            owner = lax.div(source, held * n_right)
            block = gathered[a][lax.rem(owner, 2), lax.div(owner, 2), lax.rem(source, held)]
            term = jnp.dot(block, edges_1[f, k], preferred_element_type=jnp.float32)
            total = term if total is None else total + term
        for c in range(PARTS):
            own[step + c * per_col] = total[:, c * half:(c + 1) * half]

    def piece(i, hops):
        early, late = i - LAGS[0] * hops, i - LAGS[1] * hops
        valid = ((early >= 0) & (early < per_col)) | ((late >= per_col) & (late < steps))
        return jnp.where(early < per_col, early, late), valid

    def travel(i):
        x, valid_x = piece(i, r)

        @pl.when(valid_x)
        def _():
            @pl.when(r > 0)
            def _():
                wait_bytes(prefix.at[x], right_recv.at[x])

            @pl.when(r < n_right - 1)
            def _():
                to_right[x] = (prefix[x].astype(jnp.float32) + own[x]).astype(jnp.bfloat16)
                pltpu.make_async_remote_copy(
                    src_ref=to_right.at[x], dst_ref=prefix.at[x],
                    send_sem=right_send, recv_sem=right_recv.at[x],
                    device_id=(l, r + 1), device_id_type=MESH).start()

        y, valid_y = piece(i, n_right - 1 - r)

        @pl.when(valid_y)
        def _():
            @pl.when(r < n_right - 1)
            def _():
                wait_bytes(suffix.at[y], left_recv.at[y])

            @pl.when(r > 0)
            def _():
                to_left[y] = (suffix[y].astype(jnp.float32) + own[y]).astype(jnp.bfloat16)
                pltpu.make_async_remote_copy(
                    src_ref=to_left.at[y], dst_ref=suffix.at[y],
                    send_sem=left_send, recv_sem=left_recv.at[y],
                    device_id=(l, r - 1), device_id_type=MESH).start()

        t, valid_t = piece(i, n_right - 1)

        @pl.when(valid_t)
        def _():
            c, a, f = t // per_col, (t // sectors) % PARTS, t % sectors
            whole = prefix[t].astype(jnp.float32) + own[t] + suffix[t].astype(jnp.float32)
            row_sum[f, a] = whole.astype(jnp.bfloat16)

            @pl.when(a == PARTS - 1)
            def _():
                value = jnp.dot(
                    projs_1[f], row_sum[f].reshape(size, half),
                    preferred_element_type=jnp.float32)
                absorbed[c, f] = value.astype(jnp.bfloat16)

    def column_sum(c, g, ks):
        total = None
        for k in ks:
            block = absorbed[c, lax.rem(source_col[g, k], sectors)]
            term = jnp.dot(edges_2[g, k], block, preferred_element_type=jnp.float32)
            total = term if total is None else total + term
        return total

    def column_send(c, g, total):
        col_part[c, g] = total.astype(jnp.bfloat16).reshape(n_left, size // n_left, half)
        for off in range(1, n_left):
            there = lax.rem(l + off, n_left)
            pltpu.make_async_remote_copy(
                src_ref=col_part.at[c, g, there], dst_ref=col_in.at[c, g, l],
                send_sem=col_send, recv_sem=col_recv.at[c, g],
                device_id=(there, r), device_id_type=MESH).start()
        col_in[c, g, l] = col_part[c, g, l]

    load_1.wait()

    @pl.loop(0, sectors)
    def _(f):
        projs_1[f] = projs_1[f].T

    forward(0)
    pair_copy(0).wait_recv()

    @pl.loop(0, sectors)
    def _(i):
        row_product(i, 0)
        travel(i)

        @pl.when(i == sectors // 2)
        def _():
            forward(1)

    pair_copy(1).wait_recv()

    @pl.loop(sectors, per_col)
    def _(i):
        row_product(i, 1)
        travel(i)

    first = per_col + LAGS[0] * (n_right - 1)
    cuts = [entries_2 * n // SLICES for n in range(SLICES + 1)]

    @pl.loop(per_col, steps + LAGS[1] * (n_right - 1))
    def _(i):
        travel(i)
        turn = i - first

        for n in range(SLICES):
            @pl.when((turn >= 0) & (turn < SLICES * groups) & (turn % SLICES == n))
            def _():
                g = turn // SLICES
                if n == 0:
                    wait_bytes(edges_2.at[g], edge_sem_2.at[g])
                total = column_sum(0, g, range(cuts[n], cuts[n + 1]))
                if n > 0:
                    total = total + col_total[...]
                if n < SLICES - 1:
                    col_total[...] = total
                else:
                    column_send(0, g, total)

    @pl.loop(0, groups)
    def _(g):
        column_send(1, g, column_sum(1, g, range(entries_2)))

    for o in range(mine):
        for c in range(PARTS):
            absorbed_out[o, :, c * half:(c + 1) * half] = absorbed[c, r * mine + o]

    load_2.wait()

    @pl.loop(0, groups)
    def _(g):
        parts = []
        for c in range(PARTS):
            wait_bytes(col_in.at[c, g, pl.ds(0, n_left - 1)], col_recv.at[c, g])
            parts.append(jnp.sum(col_in[c, g].astype(jnp.float32), axis=0).astype(jnp.bfloat16))
        corner_out[g] = jnp.dot(
            jnp.concatenate(parts, axis=1), projs_2[g], preferred_element_type=jnp.float32
        ).astype(jnp.bfloat16)

    for a in range(PARTS):
        if chips > 1:
            wait_bytes(gathered[a].at[0, pl.ds(0, chips - 1)], peer_send.at[a])
        pair_copy(a).wait_send()

    @pl.when(r < n_right - 1)
    def _():
        wait_bytes(to_right, right_send)

    @pl.when(r > 0)
    def _():
        wait_bytes(to_left, left_send)

    wait_bytes(col_part.at[:, :, pl.ds(0, n_left - 1)], col_send)


def hand_over(a, b, a_out, b_out, a_held, b_held, sem):
    loads = [
        pltpu.make_async_copy(a, a_held, sem.at[0]), pltpu.make_async_copy(b, b_held, sem.at[1])]
    stores = [
        pltpu.make_async_copy(a_held, a_out, sem.at[2]), pltpu.make_async_copy(b_held, b_out, sem.at[3])]
    for load in loads:
        load.start()
    for load, store in zip(loads, stores):
        load.wait()
        store.start()
    for store in stores:
        store.wait()


def body(n_left, n_right, corner, edge_row, source_row, proj_row, edge_col, source_col, proj_col):
    held, size, _ = corner.shape
    sectors, entries_1 = source_row.shape
    groups, entries_2 = source_col.shape
    half = size // PARTS
    chips = n_left // 2
    steps = PARTS * PARTS * sectors
    rows = size // n_left
    bf16 = jnp.bfloat16
    dma = pltpu.SemaphoreType.DMA
    vmem = pl.BlockSpec(memory_space=pltpu.VMEM)
    smem = pl.BlockSpec(memory_space=pltpu.SMEM)
    far = pl.BlockSpec(memory_space=pl.ANY)
    gathered = pltpu.VMEM((2, chips, held, half, size), bf16)
    pieces = pltpu.VMEM((steps, half, half), bf16)
    columns = pltpu.VMEM((PARTS, groups, n_left, rows, half), bf16)
    found = pl.pallas_call(
        functools.partial(kernel, n_left, n_right),
        out_shape=(
            jax.ShapeDtypeStruct((sectors // n_right, size, size), bf16),
            jax.ShapeDtypeStruct((groups, rows, size), bf16),
        ),
        in_specs=[smem, smem, far, far, far, far, far],
        out_specs=(vmem, vmem),
        scratch_shapes=[
            gathered, gathered,
            pltpu.VMEM(edge_row.shape, bf16), pltpu.VMEM(edge_col.shape, bf16),
            pltpu.VMEM(proj_row.shape, bf16), pltpu.VMEM(proj_col.shape, bf16),
            pltpu.VMEM((steps, half, half), jnp.float32),
            pieces, pieces, pieces, pieces,
            pltpu.VMEM((sectors, PARTS, half, half), bf16),
            pltpu.VMEM((PARTS, sectors, size, half), bf16),
            pltpu.VMEM((size, half), jnp.float32),
            columns, columns,
            dma((sectors,)), dma((groups,)), dma((2,)), dma((PARTS,)),
            dma((PARTS,)), dma((PARTS,)), dma((PARTS,)), dma((PARTS,)),
            dma, dma((steps,)), dma, dma((steps,)), dma, dma((PARTS, groups)),
        ],
        compiler_params=pltpu.CompilerParams(
            collective_id=0, has_side_effects=True, vmem_limit_bytes=58 * 2**20),
        cost_estimate=pl.CostEstimate(
            flops=2 * size**3 * (sectors * (entries_1 + 1) + groups * (entries_2 + 1)),
            bytes_accessed=2 * (edge_row.size + edge_col.size + proj_row.size + proj_col.size),
            transcendentals=0),
    )(source_row, source_col, corner, edge_row, proj_row, edge_col, proj_col)
    return pl.pallas_call(
        hand_over,
        out_shape=tuple(jax.ShapeDtypeStruct(x.shape, x.dtype) for x in found),
        in_specs=[far, far],
        out_specs=(far, far),
        scratch_shapes=[pltpu.VMEM(x.shape, x.dtype) for x in found] + [dma((4,))],
        compiler_params=pltpu.CompilerParams(vmem_limit_bytes=58 * 2**20),
        cost_estimate=pl.CostEstimate(
            flops=0, bytes_accessed=4 * sum(x.size for x in found), transcendentals=0),
    )(*found)


def solution(mesh):
    in_specs = (
        P(("left", "right"), None, None),
        P("left", "right", None, None),
        P("left", "right"),
        P("left", None, None),
        P("right", "left", None, None),
        P("right", "left"),
        P("right", None, None),
    )
    out_specs = (P(("left", "right"), None, None), P("right", "left", None))
    return jax.shard_map(
        functools.partial(body, mesh.shape["left"], mesh.shape["right"]),
        mesh=mesh, in_specs=in_specs, out_specs=out_specs, check_vma=False)
```

```python
import functools

import jax
import jax.numpy as jnp
from jax import lax
from jax.experimental import pallas as pl
from jax.experimental.pallas import tpu as pltpu
from jax.sharding import PartitionSpec as P

MESH = pl.DeviceIdType.MESH
PARTS = 2
LAGS = (4, 6)
SLICES = 2


def wait_bytes(ref, sem):
    pltpu.make_async_copy(ref, ref, sem).wait()


def kernel(
    n_left, n_right,
    source_row, source_col, corner, edge_row, proj_row, edge_col, proj_col,
    absorbed_out, corner_out,
    gathered_0, gathered_1, edges_1, edges_2, projs_1, projs_2,
    own, prefix, suffix, to_right, to_left, row_sum, absorbed, col_total, col_part, col_in,
    edge_sem_1, edge_sem_2, proj_sem, local_sem,
    peer_send, peer_recv, pair_send, pair_recv,
    right_send, right_recv, left_send, left_recv, col_send, col_recv,
):
    held = corner.shape[0]
    size = corner.shape[1]
    half = size // PARTS
    sectors, entries_1 = source_row.shape
    groups, entries_2 = source_col.shape
    mine = absorbed_out.shape[0]
    chips = n_left // 2
    per_col = PARTS * sectors
    steps = PARTS * per_col
    l, r = lax.axis_index("left"), lax.axis_index("right")
    core, chip = lax.rem(l, 2), lax.div(l, 2)
    gathered = (gathered_0, gathered_1)

    corner_copies = [
        pltpu.make_async_copy(
            corner.at[:, pl.ds(a * half, half), :], gathered[a].at[core, chip], local_sem.at[a])
        for a in range(PARTS)
    ]
    for copy in corner_copies:
        copy.start()

    load_1 = pltpu.make_async_copy(proj_row, projs_1, proj_sem.at[0])
    load_1.start()

    def load_edges(f):
        pltpu.make_async_copy(edge_row.at[f], edges_1.at[f], edge_sem_1.at[f]).start()

    for f in range(2):
        load_edges(f)

    barrier = pltpu.get_barrier_semaphore()
    for off in range(1, n_left):
        pl.semaphore_signal(
            barrier, inc=1, device_id=(lax.rem(l + off, n_left), r), device_id_type=MESH)

    @pl.when(r > 0)
    def _():
        pl.semaphore_signal(barrier, inc=1, device_id=(l, r - 1), device_id_type=MESH)

    @pl.when(r < n_right - 1)
    def _():
        pl.semaphore_signal(barrier, inc=1, device_id=(l, r + 1), device_id_type=MESH)

    pl.semaphore_wait(
        barrier,
        n_left - 1 + jnp.where(r > 0, 1, 0) + jnp.where(r < n_right - 1, 1, 0))

    def gather(a):
        for off in range(1, chips):
            peer = lax.rem(chip + off, chips)
            pltpu.make_async_remote_copy(
                src_ref=corner.at[:, pl.ds(a * half, half), :],
                dst_ref=gathered[a].at[core, chip],
                send_sem=peer_send.at[a], recv_sem=peer_recv.at[a],
                device_id=(peer * 2 + core, r), device_id_type=MESH).start()

    def pair_copy(a):
        return pltpu.make_async_remote_copy(
            src_ref=gathered[a].at[core], dst_ref=gathered[a].at[core],
            send_sem=pair_send.at[a], recv_sem=pair_recv.at[a],
            device_id=(chip * 2 + 1 - core, r), device_id_type=MESH)

    def forward(a):
        corner_copies[a].wait()
        if chips > 1:
            wait_bytes(gathered[a].at[0, pl.ds(0, chips - 1)], peer_recv.at[a])
        pair_copy(a).start()

    gather(0)

    @pl.loop(2, sectors)
    def _(f):
        load_edges(f)

    @pl.when(r == 0)
    def _():
        prefix[...] = jnp.zeros_like(prefix)

    @pl.when(r == n_right - 1)
    def _():
        suffix[...] = jnp.zeros_like(suffix)

    def row_product(step, a):
        f = step - a * sectors
        if a == 0:
            wait_bytes(edges_1.at[f], edge_sem_1.at[f])
        total = None
        for k in range(entries_1):
            source = source_row[f, k]
            owner = lax.div(source, held * n_right)
            block = gathered[a][lax.rem(owner, 2), lax.div(owner, 2), lax.rem(source, held)]
            term = jnp.dot(block, edges_1[f, k], preferred_element_type=jnp.float32)
            total = term if total is None else total + term
        for c in range(PARTS):
            own[step + c * per_col] = total[:, c * half:(c + 1) * half]

    def piece(i, hops):
        early, late = i - LAGS[0] * hops, i - LAGS[1] * hops
        valid = ((early >= 0) & (early < per_col)) | ((late >= per_col) & (late < steps))
        return jnp.where(early < per_col, early, late), valid

    def travel(i):
        x, valid_x = piece(i, r)

        @pl.when(valid_x)
        def _():
            @pl.when(r > 0)
            def _():
                wait_bytes(prefix.at[x], right_recv.at[x])

            @pl.when(r < n_right - 1)
            def _():
                to_right[x] = (prefix[x].astype(jnp.float32) + own[x]).astype(jnp.bfloat16)
                pltpu.make_async_remote_copy(
                    src_ref=to_right.at[x], dst_ref=prefix.at[x],
                    send_sem=right_send, recv_sem=right_recv.at[x],
                    device_id=(l, r + 1), device_id_type=MESH).start()

        y, valid_y = piece(i, n_right - 1 - r)

        @pl.when(valid_y)
        def _():
            @pl.when(r < n_right - 1)
            def _():
                wait_bytes(suffix.at[y], left_recv.at[y])

            @pl.when(r > 0)
            def _():
                to_left[y] = (suffix[y].astype(jnp.float32) + own[y]).astype(jnp.bfloat16)
                pltpu.make_async_remote_copy(
                    src_ref=to_left.at[y], dst_ref=suffix.at[y],
                    send_sem=left_send, recv_sem=left_recv.at[y],
                    device_id=(l, r - 1), device_id_type=MESH).start()

        t, valid_t = piece(i, n_right - 1)

        @pl.when(valid_t)
        def _():
            c, a, f = t // per_col, (t // sectors) % PARTS, t % sectors
            whole = prefix[t].astype(jnp.float32) + own[t] + suffix[t].astype(jnp.float32)
            row_sum[f, a] = whole.astype(jnp.bfloat16)

            @pl.when(a == PARTS - 1)
            def _():
                value = jnp.dot(
                    projs_1[f], row_sum[f].reshape(size, half),
                    preferred_element_type=jnp.float32)
                absorbed[c, f] = value.astype(jnp.bfloat16)

    def column_sum(c, g, ks):
        total = None
        for k in ks:
            block = absorbed[c, lax.rem(source_col[g, k], sectors)]
            term = jnp.dot(edges_2[g, k], block, preferred_element_type=jnp.float32)
            total = term if total is None else total + term
        return total

    def column_send(c, g, total):
        col_part[c, g] = total.astype(jnp.bfloat16).reshape(n_left, size // n_left, half)
        for off in range(1, n_left):
            there = lax.rem(l + off, n_left)
            pltpu.make_async_remote_copy(
                src_ref=col_part.at[c, g, there], dst_ref=col_in.at[c, g, l],
                send_sem=col_send, recv_sem=col_recv.at[c, g],
                device_id=(there, r), device_id_type=MESH).start()
        col_in[c, g, l] = col_part[c, g, l]

    load_1.wait()

    @pl.loop(0, sectors)
    def _(f):
        projs_1[f] = projs_1[f].T

    forward(0)
    gather(1)
    pair_copy(0).wait_recv()

    @pl.loop(0, groups)
    def _(g):
        pltpu.make_async_copy(edge_col.at[g], edges_2.at[g], edge_sem_2.at[g]).start()

    load_2 = pltpu.make_async_copy(proj_col, projs_2, proj_sem.at[1])
    load_2.start()

    @pl.loop(0, sectors)
    def _(i):
        row_product(i, 0)
        travel(i)

        @pl.when(i == sectors * 3 // 4)
        def _():
            forward(1)

    pair_copy(1).wait_recv()

    @pl.loop(sectors, per_col)
    def _(i):
        row_product(i, 1)
        travel(i)

    first = per_col + LAGS[0] * (n_right - 1)
    cuts = [entries_2 * n // SLICES for n in range(SLICES + 1)]

    @pl.loop(per_col, steps + LAGS[1] * (n_right - 1))
    def _(i):
        travel(i)
        turn = i - first

        for n in range(SLICES):
            @pl.when((turn >= 0) & (turn < SLICES * groups) & (turn % SLICES == n))
            def _():
                g = turn // SLICES
                if n == 0:
                    wait_bytes(edges_2.at[g], edge_sem_2.at[g])
                total = column_sum(0, g, range(cuts[n], cuts[n + 1]))
                if n > 0:
                    total = total + col_total[...]
                if n < SLICES - 1:
                    col_total[...] = total
                else:
                    column_send(0, g, total)

    @pl.loop(0, groups)
    def _(g):
        column_send(1, g, column_sum(1, g, range(entries_2)))

    for o in range(mine):
        for c in range(PARTS):
            absorbed_out[o, :, c * half:(c + 1) * half] = absorbed[c, r * mine + o]

    load_2.wait()

    @pl.loop(0, groups)
    def _(g):
        parts = []
        for c in range(PARTS):
            wait_bytes(col_in.at[c, g, pl.ds(0, n_left - 1)], col_recv.at[c, g])
            parts.append(jnp.sum(col_in[c, g].astype(jnp.float32), axis=0).astype(jnp.bfloat16))
        corner_out[g] = jnp.dot(
            jnp.concatenate(parts, axis=1), projs_2[g], preferred_element_type=jnp.float32
        ).astype(jnp.bfloat16)

    for a in range(PARTS):
        if chips > 1:
            wait_bytes(gathered[a].at[0, pl.ds(0, chips - 1)], peer_send.at[a])
        pair_copy(a).wait_send()

    @pl.when(r < n_right - 1)
    def _():
        wait_bytes(to_right, right_send)

    @pl.when(r > 0)
    def _():
        wait_bytes(to_left, left_send)

    wait_bytes(col_part.at[:, :, pl.ds(0, n_left - 1)], col_send)


def hand_over(a, b, a_out, b_out, a_held, b_held, sem):
    loads = [
        pltpu.make_async_copy(a, a_held, sem.at[0]), pltpu.make_async_copy(b, b_held, sem.at[1])]
    stores = [
        pltpu.make_async_copy(a_held, a_out, sem.at[2]), pltpu.make_async_copy(b_held, b_out, sem.at[3])]
    for load in loads:
        load.start()
    for load, store in zip(loads, stores):
        load.wait()
        store.start()
    for store in stores:
        store.wait()


def body(n_left, n_right, corner, edge_row, source_row, proj_row, edge_col, source_col, proj_col):
    held, size, _ = corner.shape
    sectors, entries_1 = source_row.shape
    groups, entries_2 = source_col.shape
    half = size // PARTS
    chips = n_left // 2
    steps = PARTS * PARTS * sectors
    rows = size // n_left
    bf16 = jnp.bfloat16
    dma = pltpu.SemaphoreType.DMA
    vmem = pl.BlockSpec(memory_space=pltpu.VMEM)
    smem = pl.BlockSpec(memory_space=pltpu.SMEM)
    far = pl.BlockSpec(memory_space=pl.ANY)
    gathered = pltpu.VMEM((2, chips, held, half, size), bf16)
    pieces = pltpu.VMEM((steps, half, half), bf16)
    columns = pltpu.VMEM((PARTS, groups, n_left, rows, half), bf16)
    found = pl.pallas_call(
        functools.partial(kernel, n_left, n_right),
        out_shape=(
            jax.ShapeDtypeStruct((sectors // n_right, size, size), bf16),
            jax.ShapeDtypeStruct((groups, rows, size), bf16),
        ),
        in_specs=[smem, smem, far, far, far, far, far],
        out_specs=(vmem, vmem),
        scratch_shapes=[
            gathered, gathered,
            pltpu.VMEM(edge_row.shape, bf16), pltpu.VMEM(edge_col.shape, bf16),
            pltpu.VMEM(proj_row.shape, bf16), pltpu.VMEM(proj_col.shape, bf16),
            pltpu.VMEM((steps, half, half), jnp.float32),
            pieces, pieces, pieces, pieces,
            pltpu.VMEM((sectors, PARTS, half, half), bf16),
            pltpu.VMEM((PARTS, sectors, size, half), bf16),
            pltpu.VMEM((size, half), jnp.float32),
            columns, columns,
            dma((sectors,)), dma((groups,)), dma((2,)), dma((PARTS,)),
            dma((PARTS,)), dma((PARTS,)), dma((PARTS,)), dma((PARTS,)),
            dma, dma((steps,)), dma, dma((steps,)), dma, dma((PARTS, groups)),
        ],
        compiler_params=pltpu.CompilerParams(
            collective_id=0, has_side_effects=True, vmem_limit_bytes=58 * 2**20),
        cost_estimate=pl.CostEstimate(
            flops=2 * size**3 * (sectors * (entries_1 + 1) + groups * (entries_2 + 1)),
            bytes_accessed=2 * (edge_row.size + edge_col.size + proj_row.size + proj_col.size),
            transcendentals=0),
    )(source_row, source_col, corner, edge_row, proj_row, edge_col, proj_col)
    return pl.pallas_call(
        hand_over,
        out_shape=tuple(jax.ShapeDtypeStruct(x.shape, x.dtype) for x in found),
        in_specs=[far, far],
        out_specs=(far, far),
        scratch_shapes=[pltpu.VMEM(x.shape, x.dtype) for x in found] + [dma((4,))],
        compiler_params=pltpu.CompilerParams(vmem_limit_bytes=58 * 2**20),
        cost_estimate=pl.CostEstimate(
            flops=0, bytes_accessed=4 * sum(x.size for x in found), transcendentals=0),
    )(*found)


def solution(mesh):
    in_specs = (
        P(("left", "right"), None, None),
        P("left", "right", None, None),
        P("left", "right"),
        P("left", None, None),
        P("right", "left", None, None),
        P("right", "left"),
        P("right", None, None),
    )
    out_specs = (P(("left", "right"), None, None), P("right", "left", None))
    return jax.shard_map(
        functools.partial(body, mesh.shape["left"], mesh.shape["right"]),
        mesh=mesh, in_specs=in_specs, out_specs=out_specs, check_vma=False)
```

```python
import functools

import jax
import jax.numpy as jnp
from jax import lax
from jax.experimental import pallas as pl
from jax.experimental.pallas import tpu as pltpu
from jax.sharding import PartitionSpec as P

MESH = pl.DeviceIdType.MESH
PARTS = 2
LAGS = (6, 8)
SLICES = 2


def wait_bytes(ref, sem):
    pltpu.make_async_copy(ref, ref, sem).wait()


def kernel(
    n_left, n_right,
    source_row, source_col, corner, edge_row, proj_row, edge_col, proj_col,
    absorbed_out, corner_out,
    gathered_0, gathered_1, edges_1, edges_2, projs_1, projs_2,
    own, prefix, suffix, to_right, to_left, row_sum, absorbed, col_total, col_part, col_in,
    edge_sem_1, edge_sem_2, proj_sem, local_sem,
    peer_send, peer_recv, pair_send, pair_recv,
    right_send, right_recv, left_send, left_recv, col_send, col_recv,
):
    held = corner.shape[0]
    size = corner.shape[1]
    half = size // PARTS
    sectors, entries_1 = source_row.shape
    groups, entries_2 = source_col.shape
    mine = absorbed_out.shape[0]
    chips = n_left // 2
    per_col = PARTS * sectors
    steps = PARTS * per_col
    l, r = lax.axis_index("left"), lax.axis_index("right")
    core, chip = lax.rem(l, 2), lax.div(l, 2)
    gathered = (gathered_0, gathered_1)

    corner_copies = [
        pltpu.make_async_copy(
            corner.at[:, pl.ds(a * half, half), :], gathered[a].at[core, chip], local_sem.at[a])
        for a in range(PARTS)
    ]
    for copy in corner_copies:
        copy.start()

    load_1 = pltpu.make_async_copy(proj_row, projs_1, proj_sem.at[0])
    load_1.start()

    def load_edges(f):
        pltpu.make_async_copy(edge_row.at[f], edges_1.at[f], edge_sem_1.at[f]).start()

    for f in range(2):
        load_edges(f)

    barrier = pltpu.get_barrier_semaphore()
    for off in range(1, n_left):
        pl.semaphore_signal(
            barrier, inc=1, device_id=(lax.rem(l + off, n_left), r), device_id_type=MESH)

    @pl.when(r > 0)
    def _():
        pl.semaphore_signal(barrier, inc=1, device_id=(l, r - 1), device_id_type=MESH)

    @pl.when(r < n_right - 1)
    def _():
        pl.semaphore_signal(barrier, inc=1, device_id=(l, r + 1), device_id_type=MESH)

    pl.semaphore_wait(
        barrier,
        n_left - 1 + jnp.where(r > 0, 1, 0) + jnp.where(r < n_right - 1, 1, 0))

    def gather(a):
        for off in range(1, chips):
            peer = lax.rem(chip + off, chips)
            pltpu.make_async_remote_copy(
                src_ref=corner.at[:, pl.ds(a * half, half), :],
                dst_ref=gathered[a].at[core, chip],
                send_sem=peer_send.at[a], recv_sem=peer_recv.at[a],
                device_id=(peer * 2 + core, r), device_id_type=MESH).start()

    def pair_copy(a):
        return pltpu.make_async_remote_copy(
            src_ref=gathered[a].at[core], dst_ref=gathered[a].at[core],
            send_sem=pair_send.at[a], recv_sem=pair_recv.at[a],
            device_id=(chip * 2 + 1 - core, r), device_id_type=MESH)

    def forward(a):
        corner_copies[a].wait()
        if chips > 1:
            wait_bytes(gathered[a].at[0, pl.ds(0, chips - 1)], peer_recv.at[a])
        pair_copy(a).start()

    gather(0)

    @pl.loop(2, sectors)
    def _(f):
        load_edges(f)

    @pl.when(r == 0)
    def _():
        prefix[...] = jnp.zeros_like(prefix)

    @pl.when(r == n_right - 1)
    def _():
        suffix[...] = jnp.zeros_like(suffix)

    def row_product(step, a):
        f = step - a * sectors
        if a == 0:
            wait_bytes(edges_1.at[f], edge_sem_1.at[f])
        total = None
        for k in range(entries_1):
            source = source_row[f, k]
            owner = lax.div(source, held * n_right)
            block = gathered[a][lax.rem(owner, 2), lax.div(owner, 2), lax.rem(source, held)]
            term = jnp.dot(block, edges_1[f, k], preferred_element_type=jnp.float32)
            total = term if total is None else total + term
        for c in range(PARTS):
            own[step + c * per_col] = total[:, c * half:(c + 1) * half]

    def piece(i, hops):
        early, late = i - LAGS[0] * hops, i - LAGS[1] * hops
        valid = ((early >= 0) & (early < per_col)) | ((late >= per_col) & (late < steps))
        return jnp.where(early < per_col, early, late), valid

    def travel(i):
        x, valid_x = piece(i, r)

        @pl.when(valid_x)
        def _():
            @pl.when(r > 0)
            def _():
                wait_bytes(prefix.at[x], right_recv.at[x])

            @pl.when(r < n_right - 1)
            def _():
                to_right[x] = (prefix[x].astype(jnp.float32) + own[x]).astype(jnp.bfloat16)
                pltpu.make_async_remote_copy(
                    src_ref=to_right.at[x], dst_ref=prefix.at[x],
                    send_sem=right_send, recv_sem=right_recv.at[x],
                    device_id=(l, r + 1), device_id_type=MESH).start()

        y, valid_y = piece(i, n_right - 1 - r)

        @pl.when(valid_y)
        def _():
            @pl.when(r < n_right - 1)
            def _():
                wait_bytes(suffix.at[y], left_recv.at[y])

            @pl.when(r > 0)
            def _():
                to_left[y] = (suffix[y].astype(jnp.float32) + own[y]).astype(jnp.bfloat16)
                pltpu.make_async_remote_copy(
                    src_ref=to_left.at[y], dst_ref=suffix.at[y],
                    send_sem=left_send, recv_sem=left_recv.at[y],
                    device_id=(l, r - 1), device_id_type=MESH).start()

        t, valid_t = piece(i, n_right - 1)

        @pl.when(valid_t)
        def _():
            c, a, f = t // per_col, (t // sectors) % PARTS, t % sectors
            whole = prefix[t].astype(jnp.float32) + own[t] + suffix[t].astype(jnp.float32)
            row_sum[f, a] = whole.astype(jnp.bfloat16)

            @pl.when(a == PARTS - 1)
            def _():
                value = jnp.dot(
                    projs_1[f], row_sum[f].reshape(size, half),
                    preferred_element_type=jnp.float32)
                absorbed[c, f] = value.astype(jnp.bfloat16)

    def column_sum(c, g, ks):
        total = None
        for k in ks:
            block = absorbed[c, lax.rem(source_col[g, k], sectors)]
            term = jnp.dot(edges_2[g, k], block, preferred_element_type=jnp.float32)
            total = term if total is None else total + term
        return total

    def column_send(c, g, total):
        col_part[c, g] = total.astype(jnp.bfloat16).reshape(n_left, size // n_left, half)
        for off in range(1, n_left):
            there = lax.rem(l + off, n_left)
            pltpu.make_async_remote_copy(
                src_ref=col_part.at[c, g, there], dst_ref=col_in.at[c, g, l],
                send_sem=col_send, recv_sem=col_recv.at[c, g],
                device_id=(there, r), device_id_type=MESH).start()
        col_in[c, g, l] = col_part[c, g, l]

    load_1.wait()

    @pl.loop(0, sectors)
    def _(f):
        projs_1[f] = projs_1[f].T

    forward(0)
    gather(1)
    pair_copy(0).wait_recv()

    @pl.loop(0, groups)
    def _(g):
        pltpu.make_async_copy(edge_col.at[g], edges_2.at[g], edge_sem_2.at[g]).start()

    load_2 = pltpu.make_async_copy(proj_col, projs_2, proj_sem.at[1])
    load_2.start()

    @pl.loop(0, sectors)
    def _(i):
        row_product(i, 0)
        travel(i)

        @pl.when(i == sectors * 3 // 4)
        def _():
            forward(1)

    pair_copy(1).wait_recv()

    @pl.loop(sectors, per_col)
    def _(i):
        row_product(i, 1)
        travel(i)

    first = per_col + LAGS[0] * (n_right - 1)
    cuts = [entries_2 * n // SLICES for n in range(SLICES + 1)]

    @pl.loop(per_col, steps + LAGS[1] * (n_right - 1))
    def _(i):
        travel(i)
        turn = i - first

        for n in range(SLICES):
            @pl.when((turn >= 0) & (turn < SLICES * groups) & (turn % SLICES == n))
            def _():
                g = turn // SLICES
                if n == 0:
                    wait_bytes(edges_2.at[g], edge_sem_2.at[g])
                total = column_sum(0, g, range(cuts[n], cuts[n + 1]))
                if n > 0:
                    total = total + col_total[...]
                if n < SLICES - 1:
                    col_total[...] = total
                else:
                    column_send(0, g, total)

    @pl.loop(0, groups)
    def _(g):
        column_send(1, g, column_sum(1, g, range(entries_2)))

    for o in range(mine):
        for c in range(PARTS):
            absorbed_out[o, :, c * half:(c + 1) * half] = absorbed[c, r * mine + o]

    load_2.wait()

    @pl.loop(0, groups)
    def _(g):
        parts = []
        for c in range(PARTS):
            wait_bytes(col_in.at[c, g, pl.ds(0, n_left - 1)], col_recv.at[c, g])
            parts.append(jnp.sum(col_in[c, g].astype(jnp.float32), axis=0).astype(jnp.bfloat16))
        corner_out[g] = jnp.dot(
            jnp.concatenate(parts, axis=1), projs_2[g], preferred_element_type=jnp.float32
        ).astype(jnp.bfloat16)

    for a in range(PARTS):
        if chips > 1:
            wait_bytes(gathered[a].at[0, pl.ds(0, chips - 1)], peer_send.at[a])
        pair_copy(a).wait_send()

    @pl.when(r < n_right - 1)
    def _():
        wait_bytes(to_right, right_send)

    @pl.when(r > 0)
    def _():
        wait_bytes(to_left, left_send)

    wait_bytes(col_part.at[:, :, pl.ds(0, n_left - 1)], col_send)


def hand_over(a, b, a_out, b_out, a_held, b_held, sem):
    loads = [
        pltpu.make_async_copy(a, a_held, sem.at[0]), pltpu.make_async_copy(b, b_held, sem.at[1])]
    stores = [
        pltpu.make_async_copy(a_held, a_out, sem.at[2]), pltpu.make_async_copy(b_held, b_out, sem.at[3])]
    for load in loads:
        load.start()
    for load, store in zip(loads, stores):
        load.wait()
        store.start()
    for store in stores:
        store.wait()


def body(n_left, n_right, corner, edge_row, source_row, proj_row, edge_col, source_col, proj_col):
    held, size, _ = corner.shape
    sectors, entries_1 = source_row.shape
    groups, entries_2 = source_col.shape
    half = size // PARTS
    chips = n_left // 2
    steps = PARTS * PARTS * sectors
    rows = size // n_left
    bf16 = jnp.bfloat16
    dma = pltpu.SemaphoreType.DMA
    vmem = pl.BlockSpec(memory_space=pltpu.VMEM)
    smem = pl.BlockSpec(memory_space=pltpu.SMEM)
    far = pl.BlockSpec(memory_space=pl.ANY)
    gathered = pltpu.VMEM((2, chips, held, half, size), bf16)
    pieces = pltpu.VMEM((steps, half, half), bf16)
    columns = pltpu.VMEM((PARTS, groups, n_left, rows, half), bf16)
    found = pl.pallas_call(
        functools.partial(kernel, n_left, n_right),
        out_shape=(
            jax.ShapeDtypeStruct((sectors // n_right, size, size), bf16),
            jax.ShapeDtypeStruct((groups, rows, size), bf16),
        ),
        in_specs=[smem, smem, far, far, far, far, far],
        out_specs=(vmem, vmem),
        scratch_shapes=[
            gathered, gathered,
            pltpu.VMEM(edge_row.shape, bf16), pltpu.VMEM(edge_col.shape, bf16),
            pltpu.VMEM(proj_row.shape, bf16), pltpu.VMEM(proj_col.shape, bf16),
            pltpu.VMEM((steps, half, half), jnp.float32),
            pieces, pieces, pieces, pieces,
            pltpu.VMEM((sectors, PARTS, half, half), bf16),
            pltpu.VMEM((PARTS, sectors, size, half), bf16),
            pltpu.VMEM((size, half), jnp.float32),
            columns, columns,
            dma((sectors,)), dma((groups,)), dma((2,)), dma((PARTS,)),
            dma((PARTS,)), dma((PARTS,)), dma((PARTS,)), dma((PARTS,)),
            dma, dma((steps,)), dma, dma((steps,)), dma, dma((PARTS, groups)),
        ],
        compiler_params=pltpu.CompilerParams(
            collective_id=0, has_side_effects=True, vmem_limit_bytes=58 * 2**20),
        cost_estimate=pl.CostEstimate(
            flops=2 * size**3 * (sectors * (entries_1 + 1) + groups * (entries_2 + 1)),
            bytes_accessed=2 * (edge_row.size + edge_col.size + proj_row.size + proj_col.size),
            transcendentals=0),
    )(source_row, source_col, corner, edge_row, proj_row, edge_col, proj_col)
    return pl.pallas_call(
        hand_over,
        out_shape=tuple(jax.ShapeDtypeStruct(x.shape, x.dtype) for x in found),
        in_specs=[far, far],
        out_specs=(far, far),
        scratch_shapes=[pltpu.VMEM(x.shape, x.dtype) for x in found] + [dma((4,))],
        compiler_params=pltpu.CompilerParams(vmem_limit_bytes=58 * 2**20),
        cost_estimate=pl.CostEstimate(
            flops=0, bytes_accessed=4 * sum(x.size for x in found), transcendentals=0),
    )(*found)


def solution(mesh):
    in_specs = (
        P(("left", "right"), None, None),
        P("left", "right", None, None),
        P("left", "right"),
        P("left", None, None),
        P("right", "left", None, None),
        P("right", "left"),
        P("right", None, None),
    )
    out_specs = (P(("left", "right"), None, None), P("right", "left", None))
    return jax.shard_map(
        functools.partial(body, mesh.shape["left"], mesh.shape["right"]),
        mesh=mesh, in_specs=in_specs, out_specs=out_specs, check_vma=False)
```
